128 devices in a mesh: slab: 16 (over z, x_hi, core), loop: 8 (over y, x_lo).
Axes of the slice: x: 4 (x_hi: 2, x_lo: 2; x = x_hi * 2 + x_lo), y: 4, z: 4, core: 2. Of those that a mesh axis runs over, the one named last changes fastest.
Arguments:
- doc_pool: bfloat16 [16, 8, 256, 4096], P('slab', 'loop'), may hold values from -6 to 6
- cand_owner: int32 [16, 8, 8, 1], P('slab', 'loop'), may hold values from 0 to 15; in each aligned block of 8 rows (0 to 7, 8 to 15, ..., all dimensions but the last counted through in order) at most 2 rows name the same one
- cand_row: int32 [16, 8, 8], P('slab', 'loop'), may hold values from 0 to 255
- elements: bfloat16 [16, 8, 2048, 4096], P('slab', 'loop'), may hold values from -6 to 6
- coverage: float32 [16, 8, 2048], P('slab', 'loop'), may hold values from -0.5 to 1.5
- elem_weight: float32 [16, 8, 2048], P('slab', 'loop'), may hold values from 1 to 10
Outputs:
- gains: float32 [16, 8, 8], P('slab', 'loop')
The draws below stay inside these ranges and needn't reach their ends.
Inputs may be any that keep to these rules, and one draw needn't show every extreme that they name: `cand_owner`: among the candidates of one device, at most 2 name the same owner; some owner is named exactly 2 times.
All inputs are finite; a program needn't handle non-finite values.
Results may differ from the reference program's by a relative error of at most 0.0003.
Values may be sent and summed in bfloat16 or wider, within the bound.
No kernel may reach another device: no remote copies, remote signals or barrier semaphores. Data moves between devices by JAX's collectives and lax.ppermute only.
A program may use at most 128 MiB of HBM per device.

```python
import math
import jax
import jax.numpy as jnp
import numpy as np
from jax import lax

D = 4096
CB = 128
ELEM_DEV = 2048
POOL_DEV = 256
CAP = 2
ELEMS = 262144
N_SLAB = 16
N_LOOP = 8


def plant(drawn, key, least, largest):
    extent = drawn.shape
    index_at = [jax.random.randint(jax.random.fold_in(key, axis), (), 0, extent[axis]) for axis in range(len(extent))]
    drawn = drawn.at[tuple(index_at)].set(least)
    longest = extent.index(max(extent))
    index_at[longest] = (index_at[longest] + 1) % extent[longest]
    return drawn.at[tuple(index_at)].set(largest)


def level_of(rng, extent, cuts, smallest, top_value):
    def one(axis_at, parts):
        heights = jax.random.uniform(jax.random.fold_in(jax.random.fold_in(rng, 6), axis_at), (parts,), jnp.float32, smallest / len(cuts), top_value / len(cuts))
        return jnp.repeat(jnp.exp(heights), extent[axis_at] // parts).reshape((-1,) + (1,) * (len(extent) - axis_at - 1))

    factor_of = one(*cuts[0])
    for cut in cuts[1:]:
        factor_of = factor_of * one(*cut)
    return factor_of


def deal_out(key, own, number, rows, count, top, most, skew):
    ranking = jax.random.permutation(key, count)
    packed, common = portions_of(count, rows * top, most, skew, True), portions_of(count, rows * top, most, skew, False)
    places = jnp.arange(count)

    def named(lengths, rotation):
        used = int((lengths > 0).sum())
        fixed = max(1, used // 4)
        shifted = fixed + (places - fixed + rotation * (used - fixed)) % max(1, count - fixed)
        return jnp.zeros((count,), jnp.int32).at[ranking[jnp.where(places < fixed, places, shifted)]].set(jnp.asarray(lengths, jnp.int32))

    lengths = jnp.where(number % 4 == 0, named(packed, number // 4), named(common, number - number // 4 - 1))
    mixed = jax.random.permutation(jax.random.fold_in(own, 3), count)
    source_of, taker = mixed[0:count // 2 * 2:2], mixed[1:count // 2 * 2:2]
    margin = jnp.minimum(lengths[source_of] - 1, most - lengths[taker]) // 2
    margin = jnp.where((source_of == ranking[0]) | (taker == ranking[0]) | (lengths[taker] == 0), 0, jnp.maximum(margin, 0))
    shifted = jax.random.randint(jax.random.fold_in(own, 4), (count // 2,), 0, 1 << 20) % (margin + 1)
    lengths = lengths.at[source_of].add(-shifted).at[taker].add(shifted)
    labels = jnp.searchsorted(jnp.cumsum(lengths), jnp.arange(rows * top), side="right").astype(jnp.int32)
    table = labels.reshape(top, rows).T
    table = table[jax.random.permutation(jax.random.fold_in(own, 1), rows)]
    rotation = jax.random.randint(jax.random.fold_in(own, 2), (rows, 1), 0, top)
    return jnp.take_along_axis(table, (jnp.arange(top)[None, :] + rotation) % top, axis=1)


def portions_of(amount, total, bound, lean, full):
    weights = [(1 << 20) // math.isqrt(standing ** lean) + 1 for standing in range(1, amount + 1)]
    largest = bound if full else min(bound, max(-(-total // amount), total * weights[0] // sum(weights)))
    least = 1 if total - largest >= amount - 1 else 0
    holding, rest = [largest] + [least] * (amount - 1), total - largest - least * (amount - 1)
    while rest > 0:
        candidates = [i for i in range(1, amount) if holding[i] < largest] or [i for i in range(1, amount) if holding[i] < bound]
        pool, budget = sum([weights[i] for i in candidates]), rest
        for i in candidates:
            extra = min(bound - holding[i], max(1, budget * weights[i] // pool), rest)
            holding[i] = holding[i] + extra
            rest = rest - extra
    return np.array(holding)


def centred(stream_key, extent, width, bound, pieces=(), kind=jnp.bfloat16):
    gain = level_of(stream_key, extent, pieces, -0.22, 0.18) if pieces else 1.0
    values = jax.random.normal(stream_key, extent, jnp.float32) * width * gain
    return jnp.minimum(jnp.maximum(values, -bound), bound).astype(kind)


def setup_inputs(seed: int = 0) -> dict:
    key_of = jax.random.split(jax.random.key(seed), 7)
    doc_pool = centred(key_of[0], (N_SLAB, N_LOOP, POOL_DEV, D), 1.0, 6.0, ((0, 16), (1, 8)))
    cand_owner_keys = jax.random.split(jax.random.fold_in(key_of[1], 1), N_SLAB * N_LOOP * (CB // N_SLAB) // (CB // N_SLAB))
    cand_owner_turns = jax.random.permutation(jax.random.fold_in(key_of[1], 3), N_SLAB * N_LOOP * (CB // N_SLAB) // (CB // N_SLAB))
    cand_owner = jax.vmap(lambda own, number: deal_out(jax.random.fold_in(key_of[1], 2), own, number, CB // N_SLAB, N_SLAB, 1, CAP, 2))(cand_owner_keys, cand_owner_turns).reshape((N_SLAB, N_LOOP, CB // N_SLAB, 1))
    cand_row = plant(jax.random.randint(key_of[2], (N_SLAB, N_LOOP, CB // N_SLAB), 0, POOL_DEV), jax.random.fold_in(key_of[2], 1), 0, POOL_DEV - 1).astype(jnp.int32)
    elements = centred(key_of[3], (N_SLAB, N_LOOP, ELEM_DEV, D), 1.0, 6.0, ((0, 16), (1, 8)))
    coverage = jnp.clip(-0.5 + 2.0 * jax.random.uniform(key_of[4], (N_SLAB, N_LOOP, ELEM_DEV), jnp.float32) ** level_of(key_of[4], (N_SLAB, N_LOOP, ELEM_DEV), ((0, 16), (1, 8)), -0.2, 0.2), -0.5, 1.5)
    elem_weight = jnp.clip(jnp.exp(math.log(10.0) - 2.3025851 * jax.random.uniform(key_of[5], (N_SLAB, N_LOOP, ELEM_DEV), jnp.float32) ** level_of(key_of[5], (N_SLAB, N_LOOP, ELEM_DEV), ((0, 16), (1, 8)), -0.2, 0.2)), 1.0, 10.0)
    return dict(doc_pool=doc_pool, cand_owner=cand_owner, cand_row=cand_row, elements=elements, coverage=coverage, elem_weight=elem_weight)


def reference(doc_pool, cand_owner, cand_row, elements, coverage, elem_weight):
    owner_ids = cand_owner[..., 0]
    column_ids = jnp.broadcast_to(jnp.arange(N_LOOP, dtype=jnp.int32)[None, :, None], owner_ids.shape)
    cand_emb = doc_pool[owner_ids, column_ids, cand_row]
    cand_flat = cand_emb.reshape(-1, D)
    sim_scale = float(D) ** -0.5
    shard_elems = elements.reshape(N_SLAB * N_LOOP, ELEM_DEV, D)
    shard_cover = coverage.reshape(N_SLAB * N_LOOP, ELEM_DEV)
    shard_weight = elem_weight.reshape(N_SLAB * N_LOOP, ELEM_DEV)

    def accumulate(running, shard):
        docs, cover_part, weight_part = shard
        scores = jnp.dot(docs, cand_flat.T, preferred_element_type=jnp.float32) * sim_scale
        term = jnp.sum(weight_part[:, None] * jnp.maximum(scores - cover_part[:, None], 0.0), axis=0)
        return running + term, None

    init = jnp.zeros((cand_flat.shape[0],), jnp.float32)
    running, _ = lax.scan(accumulate, init, (shard_elems, shard_cover, shard_weight))
    gains = running / float(ELEMS)
    return gains.reshape(owner_ids.shape)
```

```python
import functools

import jax
import jax.numpy as jnp
from jax import lax
from jax.experimental import pallas as pl
from jax.experimental.pallas import tpu as pltpu
from jax.sharding import PartitionSpec as P

AXES = ("slab", "loop")
RING = 4
TILE = 512


def place(index):
    slab, loop = divmod(index, 8)
    z, rest = divmod(slab, 4)
    hi, core = divmod(rest, 2)
    y, lo = divmod(loop, 2)
    return z, hi * 2 + lo, y, core


def index_of(z, x, y, core):
    return ((z * 2 + x // 2) * 2 + core) * 8 + y * 2 + x % 2


def moves(dz=0, dx=0, dy=0, dc=0):
    pairs = []
    for source in range(128):
        z, x, y, core = place(source)
        pairs.append((source, index_of((z + dz) % RING, (x + dx) % RING, (y + dy) % RING, core ^ dc)))
    return pairs


def send(value, **step):
    return lax.ppermute(value, AXES, moves(**step))


def add_terms(cand, docs, cw, out_ref, start, doc_at):
    scores = lax.dot_general(
        cand[...], docs[pl.ds(start, TILE), :], (((1,), (1,)), ((), ())), preferred_element_type=jnp.float32
    )
    cover = cw[0:1, pl.ds(doc_at, TILE)]
    weight = cw[1:2, pl.ds(doc_at, TILE)]
    term = weight * jnp.maximum(scores - cover, 0.0)
    total = out_ref[...]
    for j in range(TILE // 128):
        total = total + term[:, j * 128 : (j + 1) * 128]
    out_ref[...] = total


def pack(pieces, cand):
    at = 0
    for piece in pieces:
        rows = piece.shape[0]
        cand[at : at + rows, :] = piece[...]
        at += rows


def first_kernel(count, *refs):
    pieces = refs[:count]
    own_hbm, sib_hbm, own_cw, sib_cw, out_ref, own_docs, sib_docs, cand, arrived = refs[count:]
    steps = own_hbm.shape[0] // TILE

    def copy(i, source, target, base):
        rows = pl.ds(pl.multiple_of(i * TILE, TILE), TILE)
        return pltpu.make_async_copy(source.at[rows], target.at[rows], arrived.at[base + i])

    for i in range(steps):
        copy(i, own_hbm, own_docs, 0).start()
    for i in range(steps):
        copy(i, sib_hbm, sib_docs, steps).start()
    pack(pieces, cand)
    out_ref[...] = jnp.zeros_like(out_ref)
    for source, docs, cw, base in ((own_hbm, own_docs, own_cw, 0), (sib_hbm, sib_docs, sib_cw, steps)):

        def step(i, carry, source=source, docs=docs, cw=cw, base=base):
            copy(i, source, docs, base).wait()
            start = pl.multiple_of(i * TILE, TILE)
            add_terms(cand, docs, cw, out_ref, start, start)
            return carry

        lax.fori_loop(0, steps, step, 0)


def later_kernel(count, *refs):
    pieces = refs[:count]
    own_docs, sib_docs, own_cw, sib_cw, out_ref, cand = refs[count:]
    pack(pieces, cand)
    out_ref[...] = jnp.zeros_like(out_ref)
    for docs, cw in ((own_docs, own_cw), (sib_docs, sib_cw)):

        def step(i, carry, docs=docs, cw=cw):
            start = pl.multiple_of(i * TILE, TILE)
            add_terms(cand, docs, cw, out_ref, start, start)
            return carry

        lax.fori_loop(0, docs.shape[0] // TILE, step, 0)


def gains_of(pieces, own_docs, sib_docs, own_cw, sib_cw, name, first=False):
    count = len(pieces)
    rows, width = sum(p.shape[0] for p in pieces), own_docs.shape[1]
    docs = own_docs.shape[0] + sib_docs.shape[0]
    in_vmem = pl.BlockSpec(memory_space=pltpu.VMEM)
    in_hbm = pl.BlockSpec(memory_space=pltpu.HBM)
    out_shape = [jax.ShapeDtypeStruct((rows, 128), jnp.float32)]
    scratch = [pltpu.VMEM((rows, width), jnp.bfloat16)]
    if first:
        out_shape += [pltpu.VMEM(own_docs.shape, own_docs.dtype), pltpu.VMEM(sib_docs.shape, sib_docs.dtype)]
        scratch += [pltpu.SemaphoreType.DMA((docs // TILE,))]
    return pl.pallas_call(
        functools.partial(first_kernel if first else later_kernel, count),
        in_specs=[in_vmem] * count + [in_hbm if first else in_vmem] * 2 + [in_vmem] * 2,
        out_specs=[in_vmem] * len(out_shape),
        out_shape=out_shape,
        scratch_shapes=scratch,
        compiler_params=pltpu.CompilerParams(vmem_limit_bytes=8 * 2**20),
        cost_estimate=pl.CostEstimate(
            flops=2 * docs * rows * width, bytes_accessed=docs * width * 2 if first else 0, transcendentals=0
        ),
        name=name,
    )(*pieces, own_docs, sib_docs, own_cw, sib_cw)


def body(doc_pool, cand_owner, cand_row, elements, coverage, elem_weight):
    share_len = cand_row.shape[2]
    width = doc_pool.shape[3]
    slab_count = 16
    slot_cap = 2
    pool_local = doc_pool.reshape(doc_pool.shape[2], width)
    owner_ids = cand_owner.reshape(share_len)
    row_ids = cand_row.reshape(share_len)
    docs = elements.reshape(elements.shape[2], width)
    scale_up = float(width) ** 0.5
    element_total = float(docs.shape[0] * 128)
    cw = jnp.stack(
        [coverage.reshape(-1) * scale_up, elem_weight.reshape(-1) * (1.0 / (scale_up * element_total))]
    )
    sib_docs = send(docs, dc=1)
    sib_cw = send(cw, dc=1)

    positions = jnp.arange(share_len, dtype=jnp.int32)
    same_owner = owner_ids[:, None] == owner_ids[None, :]
    earlier = positions[None, :] < positions[:, None]
    slot_rank = jnp.sum((same_owner & earlier).astype(jnp.int32), axis=1)
    slot_id = owner_ids * slot_cap + slot_rank
    onehot = (
        slot_id[:, None] == jnp.arange(slab_count * slot_cap, dtype=jnp.int32)[None, :]
    ).astype(jnp.int32)
    requests = jnp.sum(onehot * row_ids[:, None], axis=0).reshape(slab_count, slot_cap)
    asked = lax.all_to_all(requests, "slab", split_axis=0, concat_axis=0, tiled=True)
    doc_rows = pool_local.at[asked.reshape(-1)].get(mode="promise_in_bounds")
    fetched = lax.all_to_all(
        doc_rows.reshape(slab_count, slot_cap, width), "slab", split_axis=0, concat_axis=0, tiled=True
    )
    own = fetched.reshape(slab_count * slot_cap, width).at[slot_id].get(mode="promise_in_bounds")

    z3, z1, z2 = send(own, dz=1), send(own, dz=-1), send(own, dz=2)
    part_a = jnp.concatenate([own, z1], axis=0)
    part_b = jnp.concatenate([z2, z3], axis=0)
    a3, a1, a2 = send(part_a, dx=1), send(part_a, dx=-1), send(part_a, dx=2)
    b3, b1, b2 = send(part_b, dy=1), send(part_b, dy=-1), send(part_b, dy=2)
    block_a = jnp.concatenate([part_a, a1, a2, a3], axis=0)
    block_b = jnp.concatenate([part_b, b1, b2, b3], axis=0)
    aa3, aa1 = send(block_a, dy=1), send(block_a, dy=-1)
    bb3, bb1 = send(block_b, dx=1), send(block_b, dx=-1)
    g0, own_here, sib_here = gains_of(
        [block_a, block_b], docs, sib_docs, cw, sib_cw, "gains_near", first=True
    )
    far_a, far_b, aa1, aa3, bb1, bb3 = lax.optimization_barrier((block_a, block_b, aa1, aa3, bb1, bb3))
    aa2, bb2 = send(far_a, dy=2), send(far_b, dx=2)
    (g1,) = gains_of([aa1, aa3, bb1, bb3], own_here, sib_here, cw, sib_cw, "gains_next")
    cw, g1 = lax.optimization_barrier((cw, g1))
    (g2,) = gains_of([aa2, bb2], own_here, sib_here, cw, sib_cw, "gains_far")
    g0, g1, g2 = jnp.sum(g0, axis=1), jnp.sum(g1, axis=1), jnp.sum(g2, axis=1)
    n = block_a.shape[0]
    gain_a = jnp.stack([g0[:n], g1[:n], g2[:n], g1[n : 2 * n]])
    gain_b = jnp.stack([g0[n:], g1[2 * n : 3 * n], g2[n:], g1[3 * n :]])
    gain_a = gain_a.reshape(RING, RING, 2, share_len)
    gain_b = gain_b.reshape(RING, RING, 2, share_len).transpose(1, 0, 2, 3)
    gains = jnp.concatenate([gain_a, gain_b], axis=2).reshape(64, share_len)

    slab, loop = lax.axis_index("slab"), lax.axis_index("loop")
    my_z, my_x, my_y = slab >> 2, (slab & 2) + (loop & 1), loop >> 1
    to = jnp.arange(64, dtype=jnp.int32)
    to_z, to_x, to_y = to >> 4, ((to >> 2) & 2) + (to & 1), (to >> 1) & 3
    rel = ((to_y - my_y) & 3) * 16 + ((to_x - my_x) & 3) * 4 + ((to_z - my_z) & 3)
    pick = rel[:, None] == jnp.arange(64, dtype=jnp.int32)[None, :]
    terms = jnp.sum(jnp.where(pick[:, :, None], gains[None, :, :], 0.0), axis=1)
    groups = [[i for i in range(128) if place(i)[3] == core] for core in range(2)]
    terms = lax.all_to_all(terms, AXES, split_axis=0, concat_axis=0, tiled=True, axis_index_groups=groups)
    return jnp.sum(terms, axis=0).reshape(1, 1, share_len)


def solution(mesh):
    placed = (
        P("slab", "loop", None, None),
        P("slab", "loop", None, None),
        P("slab", "loop", None),
        P("slab", "loop", None, None),
        P("slab", "loop", None),
        P("slab", "loop", None),
    )
    return jax.shard_map(
        body, mesh=mesh, in_specs=placed, out_specs=P("slab", "loop", None), check_vma=False
    )
```

```python
import functools

import jax
import jax.numpy as jnp
from jax import lax
from jax.experimental import pallas as pl
from jax.experimental.pallas import tpu as pltpu
from jax.sharding import PartitionSpec as P

AXES = ("slab", "loop")
RING = 4
TILE = 512


def place(index):
    slab, loop = divmod(index, 8)
    z, rest = divmod(slab, 4)
    hi, core = divmod(rest, 2)
    y, lo = divmod(loop, 2)
    return z, hi * 2 + lo, y, core


def index_of(z, x, y, core):
    return ((z * 2 + x // 2) * 2 + core) * 8 + y * 2 + x % 2


def moves(dz=0, dx=0, dy=0, dc=0):
    pairs = []
    for source in range(128):
        z, x, y, core = place(source)
        pairs.append((source, index_of((z + dz) % RING, (x + dx) % RING, (y + dy) % RING, core ^ dc)))
    return pairs


def send(value, **step):
    return lax.ppermute(value, AXES, moves(**step))


def add_terms(cand, docs, cw, out_ref, start):
    scores = lax.dot_general(
        docs[pl.ds(start, TILE), :], cand[...], (((1,), (1,)), ((), ())), preferred_element_type=jnp.float32
    )
    columns = cw[:, pl.ds(start, TILE)].T
    term = columns[:, 1:2] * jnp.maximum(scores - columns[:, 0:1], 0.0)
    out_ref[...] += jnp.sum(term.reshape(TILE // 8, 8, term.shape[1]), axis=0)


def pack(pieces, cand):
    at = 0
    for piece in pieces:
        rows = piece.shape[0]
        cand[at : at + rows, :] = piece[...]
        at += rows


def first_kernel(count, *refs):
    pieces = refs[:count]
    own_hbm, sib_hbm, own_cw, sib_cw, out_ref, own_docs, sib_docs, cand, arrived = refs[count:]
    steps = own_hbm.shape[0] // TILE

    def copy(i, source, target, base):
        rows = pl.ds(pl.multiple_of(i * TILE, TILE), TILE)
        return pltpu.make_async_copy(source.at[rows], target.at[rows], arrived.at[base + i])

    for i in range(steps):
        copy(i, own_hbm, own_docs, 0).start()
    for i in range(steps):
        copy(i, sib_hbm, sib_docs, steps).start()
    pack(pieces, cand)
    out_ref[...] = jnp.zeros_like(out_ref)
    for source, docs, cw, base in ((own_hbm, own_docs, own_cw, 0), (sib_hbm, sib_docs, sib_cw, steps)):

        def step(i, carry, source=source, docs=docs, cw=cw, base=base):
            copy(i, source, docs, base).wait()
            start = pl.multiple_of(i * TILE, TILE)
            add_terms(cand, docs, cw, out_ref, start)
            return carry

        lax.fori_loop(0, steps, step, 0)


def later_kernel(count, *refs):
    pieces = refs[:count]
    own_docs, sib_docs, own_cw, sib_cw, out_ref, cand = refs[count:]
    pack(pieces, cand)
    out_ref[...] = jnp.zeros_like(out_ref)
    for docs, cw in ((own_docs, own_cw), (sib_docs, sib_cw)):

        def step(i, carry, docs=docs, cw=cw):
            start = pl.multiple_of(i * TILE, TILE)
            add_terms(cand, docs, cw, out_ref, start)
            return carry

        lax.fori_loop(0, docs.shape[0] // TILE, step, 0)


def gains_of(pieces, own_docs, sib_docs, own_cw, sib_cw, name, first=False):
    count = len(pieces)
    rows, width = sum(p.shape[0] for p in pieces), own_docs.shape[1]
    docs = own_docs.shape[0] + sib_docs.shape[0]
    in_vmem = pl.BlockSpec(memory_space=pltpu.VMEM)
    in_hbm = pl.BlockSpec(memory_space=pltpu.HBM)
    out_shape = [jax.ShapeDtypeStruct((8, rows), jnp.float32)]
    scratch = [pltpu.VMEM((rows, width), jnp.bfloat16)]
    if first:
        out_shape += [pltpu.VMEM(own_docs.shape, own_docs.dtype), pltpu.VMEM(sib_docs.shape, sib_docs.dtype)]
        scratch += [pltpu.SemaphoreType.DMA((docs // TILE,))]
    return pl.pallas_call(
        functools.partial(first_kernel if first else later_kernel, count),
        in_specs=[in_vmem] * count + [in_hbm if first else in_vmem] * 2 + [in_vmem] * 2,
        out_specs=[in_vmem] * len(out_shape),
        out_shape=out_shape,
        scratch_shapes=scratch,
        compiler_params=pltpu.CompilerParams(vmem_limit_bytes=8 * 2**20),
        cost_estimate=pl.CostEstimate(
            flops=5 * docs * rows * width, bytes_accessed=0, transcendentals=0
        ),
        name=name,
    )(*pieces, own_docs, sib_docs, own_cw, sib_cw)


def body(doc_pool, cand_owner, cand_row, elements, coverage, elem_weight):
    share_len = cand_row.shape[2]
    width = doc_pool.shape[3]
    slab_count = 16
    slot_cap = 2
    pool_local = doc_pool.reshape(doc_pool.shape[2], width)
    owner_ids = cand_owner.reshape(share_len)
    row_ids = cand_row.reshape(share_len)
    docs = elements.reshape(elements.shape[2], width)
    scale_up = float(width) ** 0.5
    element_total = float(docs.shape[0] * 128)
    cw = jnp.stack(
        [coverage.reshape(-1) * scale_up, elem_weight.reshape(-1) * (1.0 / (scale_up * element_total))]
    )
    cw = jnp.pad(cw, ((0, 6), (0, 0)))

    positions = jnp.arange(share_len, dtype=jnp.int32)
    same_owner = owner_ids[:, None] == owner_ids[None, :]
    earlier = positions[None, :] < positions[:, None]
    slot_rank = jnp.sum((same_owner & earlier).astype(jnp.int32), axis=1)
    slot_id = owner_ids * slot_cap + slot_rank
    onehot = (
        slot_id[:, None] == jnp.arange(slab_count * slot_cap, dtype=jnp.int32)[None, :]
    ).astype(jnp.int32)
    requests = jnp.sum(onehot * row_ids[:, None], axis=0).reshape(slab_count, slot_cap)
    asked = lax.all_to_all(requests, "slab", split_axis=0, concat_axis=0, tiled=True)
    doc_rows = pool_local.at[asked.reshape(-1)].get(mode="promise_in_bounds")
    fetched = lax.all_to_all(
        doc_rows.reshape(slab_count, slot_cap, width), "slab", split_axis=0, concat_axis=0, tiled=True
    )
    own = fetched.reshape(slab_count * slot_cap, width).at[slot_id].get(mode="promise_in_bounds")

    own, outgoing = lax.optimization_barrier((own, docs))
    sib_docs, sib_cw = send(outgoing, dc=1), send(cw, dc=1)
    z3, z1, z2 = send(own, dz=1), send(own, dz=-1), send(own, dz=2)
    part_a = jnp.concatenate([own, z1], axis=0)
    part_b = jnp.concatenate([z2, z3], axis=0)
    a3, a1, a2 = send(part_a, dx=1), send(part_a, dx=-1), send(part_a, dx=2)
    b3, b1, b2 = send(part_b, dy=1), send(part_b, dy=-1), send(part_b, dy=2)
    block_a = jnp.concatenate([part_a, a1, a2, a3], axis=0)
    block_b = jnp.concatenate([part_b, b1, b2, b3], axis=0)
    aa3, aa1 = send(block_a, dy=1), send(block_a, dy=-1)
    bb3, bb1 = send(block_b, dx=1), send(block_b, dx=-1)
    g0, own_here, sib_here = gains_of(
        [block_a, block_b], docs, sib_docs, cw, sib_cw, "gains_near", first=True
    )
    far_a, far_b, aa1, aa3, bb1, bb3, g0 = lax.optimization_barrier(
        (block_a, block_b, aa1, aa3, bb1, bb3, g0)
    )
    aa2, bb2 = send(far_a, dy=2), send(far_b, dx=2)
    (g1,) = gains_of([aa1, aa3, bb1, bb3], own_here, sib_here, cw, sib_cw, "gains_next")
    cw, g1 = lax.optimization_barrier((cw, g1))
    (g2,) = gains_of([aa2, bb2], own_here, sib_here, cw, sib_cw, "gains_far")
    g0, g1, g2 = lax.optimization_barrier((g0, g1, g2))
    g0, g1, g2 = jnp.sum(g0, axis=0), jnp.sum(g1, axis=0), jnp.sum(g2, axis=0)
    n = block_a.shape[0]
    gain_a = jnp.stack([g0[:n], g1[:n], g2[:n], g1[n : 2 * n]])
    gain_b = jnp.stack([g0[n:], g1[2 * n : 3 * n], g2[n:], g1[3 * n :]])
    gain_a = gain_a.reshape(RING, RING, 2, share_len)
    gain_b = gain_b.reshape(RING, RING, 2, share_len).transpose(1, 0, 2, 3)
    gains = jnp.concatenate([gain_a, gain_b], axis=2).reshape(64, share_len)

    slab, loop = lax.axis_index("slab"), lax.axis_index("loop")
    my_z, my_x, my_y = slab >> 2, (slab & 2) + (loop & 1), loop >> 1
    to = jnp.arange(64, dtype=jnp.int32)
    to_z, to_x, to_y = to >> 4, ((to >> 2) & 2) + (to & 1), (to >> 1) & 3
    rel = ((to_y - my_y) & 3) * 16 + ((to_x - my_x) & 3) * 4 + ((to_z - my_z) & 3)
    pick = rel[:, None] == jnp.arange(64, dtype=jnp.int32)[None, :]
    terms = jnp.sum(jnp.where(pick[:, :, None], gains[None, :, :], 0.0), axis=1)
    groups = [[i for i in range(128) if place(i)[3] == core] for core in range(2)]
    terms = lax.all_to_all(terms, AXES, split_axis=0, concat_axis=0, tiled=True, axis_index_groups=groups)
    return jnp.sum(terms, axis=0).reshape(1, 1, share_len)


def solution(mesh):
    placed = (
        P("slab", "loop", None, None),
        P("slab", "loop", None, None),
        P("slab", "loop", None),
        P("slab", "loop", None, None),
        P("slab", "loop", None),
        P("slab", "loop", None),
    )
    return jax.shard_map(
        body, mesh=mesh, in_specs=placed, out_specs=P("slab", "loop", None), check_vma=False
    )
```

```python
import functools

import jax
import jax.numpy as jnp
from jax import lax
from jax.experimental import pallas as pl
from jax.experimental.pallas import tpu as pltpu
from jax.sharding import PartitionSpec as P

AXES = ("slab", "loop")
RING = 4
TILE = 512


def place(index):
    slab, loop = divmod(index, 8)
    z, rest = divmod(slab, 4)
    hi, core = divmod(rest, 2)
    y, lo = divmod(loop, 2)
    return z, hi * 2 + lo, y, core


def index_of(z, x, y, core):
    return ((z * 2 + x // 2) * 2 + core) * 8 + y * 2 + x % 2


def moves(*steps):
    pairs = []
    for source in range(128):
        z, x, y, core = place(source)
        step = dict(steps[core % len(steps)])
        z, x, y = z + step.get("z", 0), x + step.get("x", 0), y + step.get("y", 0)
        pairs.append((source, index_of(z % RING, x % RING, y % RING, core ^ step.get("core", 0))))
    return pairs


def send(value, *steps):
    return lax.ppermute(value, AXES, moves(*steps))


def along(value, axes, distance):
    return send(value, *({axis: distance} for axis in axes))


def add_terms(cand, docs, cw, out_ref, start, doc_at):
    scores = lax.dot_general(
        docs[pl.ds(start, TILE), :], cand[...], (((1,), (1,)), ((), ())), preferred_element_type=jnp.float32
    )
    columns = cw[:, pl.ds(doc_at, TILE)].T
    term = columns[:, 1:2] * jnp.maximum(scores - columns[:, 0:1], 0.0)
    out_ref[...] += jnp.sum(term.reshape(TILE // 8, 8, term.shape[1]), axis=0)


def pack(pieces, cand):
    at = 0
    for piece in pieces:
        rows = piece.shape[0]
        cand[at : at + rows, :] = piece[...]
        at += rows


def loading_kernel(spans, held, *refs):
    count = len(spans)
    cand, sources, cws = refs[0], refs[1 : 1 + count], refs[1 + count : 1 + 2 * count]
    outs = refs[1 + 2 * count + held :]
    out_ref, loaded, arrived = outs[0], outs[1 : 1 + count], outs[1 + count :]

    def copy(part, i):
        low = spans[part][0]
        here = pl.ds(pl.multiple_of(i * TILE, TILE), TILE)
        there = pl.ds(pl.multiple_of(low + i * TILE, TILE), TILE)
        return pltpu.make_async_copy(sources[part].at[there], loaded[part].at[here], arrived[part].at[i])

    for part, (low, high) in enumerate(spans):
        for i in range((high - low) // TILE):
            copy(part, i).start()
    out_ref[...] = jnp.zeros_like(out_ref)
    for part, (low, high) in enumerate(spans):

        def step(i, carry, part=part, low=low):
            copy(part, i).wait()
            start = pl.multiple_of(i * TILE, TILE)
            add_terms(cand, loaded[part], cws[part], out_ref, start, pl.multiple_of(low + start, TILE))
            return carry

        lax.fori_loop(0, (high - low) // TILE, step, 0)


def loading_gains(cand, parts, name, held=()):
    rows, width = cand.shape
    spans = tuple((low, high) for _, low, high, _ in parts)
    docs = [pltpu.with_memory_space_constraint(part[0], pltpu.HBM) for part in parts]
    in_vmem = pl.BlockSpec(memory_space=pltpu.VMEM)
    in_hbm = pl.BlockSpec(memory_space=pltpu.HBM)
    sizes = [high - low for low, high in spans]
    return pl.pallas_call(
        functools.partial(loading_kernel, spans, len(held)),
        in_specs=[in_vmem] + [in_hbm] * len(parts) + [in_vmem] * (len(parts) + len(held)),
        out_specs=[in_vmem] * (1 + len(parts)),
        out_shape=[jax.ShapeDtypeStruct((8, rows), jnp.float32)]
        + [pltpu.VMEM((size, width), jnp.bfloat16) for size in sizes],
        scratch_shapes=[pltpu.SemaphoreType.DMA((size // TILE,)) for size in sizes],
        compiler_params=pltpu.CompilerParams(vmem_limit_bytes=8 * 2**20),
        cost_estimate=pl.CostEstimate(
            flops=5 * sum(sizes) * rows * width, bytes_accessed=0, transcendentals=0
        ),
        name=name,
    )(cand, *docs, *[part[3] for part in parts], *held)


def gain_kernel(count, lows, *refs):
    pieces = refs[:count]
    docs, cws = refs[count : count + len(lows)], refs[count + len(lows) : count + 2 * len(lows)]
    out_ref = refs[count + 2 * len(lows)]
    if count > 1:
        cand = refs[-1]
        pack(pieces, cand)
    else:
        (cand,) = pieces
    out_ref[...] = jnp.zeros_like(out_ref)
    for part, low in enumerate(lows):
        for start in range(0, docs[part].shape[0], TILE):
            add_terms(cand, docs[part], cws[part], out_ref, start, low + start)


def gains_of(pieces, parts, name):
    count = len(pieces)
    rows, width = sum(p.shape[0] for p in pieces), pieces[0].shape[1]
    docs = sum(part[0].shape[0] for part in parts)
    in_vmem = pl.BlockSpec(memory_space=pltpu.VMEM)
    return pl.pallas_call(
        functools.partial(gain_kernel, count, tuple(part[1] for part in parts)),
        in_specs=[in_vmem] * (count + 2 * len(parts)),
        out_specs=in_vmem,
        out_shape=jax.ShapeDtypeStruct((8, rows), jnp.float32),
        scratch_shapes=[pltpu.VMEM((rows, width), jnp.bfloat16)] if count > 1 else [],
        compiler_params=pltpu.CompilerParams(vmem_limit_bytes=8 * 2**20),
        cost_estimate=pl.CostEstimate(flops=5 * docs * rows * width, bytes_accessed=0, transcendentals=0),
        name=name,
    )(*pieces, *[part[0] for part in parts], *[part[2] for part in parts])


def answer_kernel(me, asked, pool_hbm, out_ref, picked, pool, arrived):
    chunks = arrived.shape[0]
    size = pool.shape[0] // chunks
    copies = [
        pltpu.make_async_copy(
            pool_hbm.at[i * size : (i + 1) * size], pool.at[i * size : (i + 1) * size], arrived.at[i]
        )
        for i in range(chunks)
    ]
    for copy in copies:
        copy.start()
    askers = asked.shape[0]
    place_of = lax.broadcasted_iota(jnp.int32, asked.shape[1:], 0) * 65536
    for a in range(askers):
        named = asked[a]
        mine = (named >> 16) == me[0]
        key = place_of + (named & 65535)
        first = jnp.min(jnp.where(mine, key, 2**30), axis=0, keepdims=True)
        last = jnp.max(jnp.where(mine, key, 0), axis=0, keepdims=True)
        picked[2 * a : 2 * a + 1, :] = first & 65535
        picked[2 * a + 1 : 2 * a + 2, :] = last & 65535
    lanes = lax.broadcasted_iota(jnp.int32, picked.shape, 1)
    rows = picked[...]
    onehot = jnp.concatenate(
        [(rows == lanes + base).astype(jnp.float32) for base in range(0, pool.shape[0], 128)], axis=1
    ).astype(jnp.bfloat16)
    for copy in copies:
        copy.wait()
    found = jnp.dot(onehot, pool[...], preferred_element_type=jnp.float32)
    for a in range(askers):
        out_ref[a] = found[2 * a : 2 * a + 2, :].astype(out_ref.dtype)


def answer(me, asked, pool):
    in_vmem = pl.BlockSpec(memory_space=pltpu.VMEM)
    askers, width = asked.shape[0], pool.shape[1]
    return pl.pallas_call(
        answer_kernel,
        in_specs=[pl.BlockSpec(memory_space=pltpu.SMEM), in_vmem, pl.BlockSpec(memory_space=pltpu.HBM)],
        out_specs=in_vmem,
        out_shape=jax.ShapeDtypeStruct((askers, 2, width), pool.dtype),
        scratch_shapes=[
            pltpu.VMEM((2 * askers, 128), jnp.int32),
            pltpu.VMEM(pool.shape, pool.dtype),
            pltpu.SemaphoreType.DMA((4,)),
        ],
        compiler_params=pltpu.CompilerParams(vmem_limit_bytes=10 * 2**20),
        name="answer",
    )(me, asked, pltpu.with_memory_space_constraint(pool, pltpu.HBM))


def body(doc_pool, cand_owner, cand_row, elements, coverage, elem_weight):
    share_len = cand_row.shape[2]
    width = doc_pool.shape[3]
    slab_count = 16
    slot_cap = 2
    pool_local = doc_pool.reshape(doc_pool.shape[2], width)
    owner_ids = cand_owner.reshape(share_len)
    row_ids = cand_row.reshape(share_len)
    docs = elements.reshape(elements.shape[2], width)
    scale_up = float(width) ** 0.5
    element_total = float(docs.shape[0] * 128)
    cw = jnp.stack(
        [coverage.reshape(-1) * scale_up, elem_weight.reshape(-1) * (1.0 / (scale_up * element_total))]
    )
    cw = jnp.pad(cw, ((0, 6), (0, 0)))

    slab, loop = lax.axis_index("slab"), lax.axis_index("loop")
    named = jnp.broadcast_to((owner_ids * 65536 + row_ids)[None, :, None], (slab_count, share_len, 128))
    asked = lax.all_to_all(named, "slab", split_axis=0, concat_axis=0, tiled=True)
    rows_out = answer(slab.reshape(1), asked, pool_local)
    rows_out, owner_ids = lax.optimization_barrier((rows_out, owner_ids))
    fetched = lax.all_to_all(rows_out, "slab", split_axis=0, concat_axis=0, tiled=True)
    positions = jnp.arange(share_len, dtype=jnp.int32)
    same_owner = owner_ids[:, None] == owner_ids[None, :]
    earlier = positions[None, :] < positions[:, None]
    slot_rank = jnp.sum((same_owner & earlier).astype(jnp.int32), axis=1)
    slot_id = owner_ids * slot_cap + slot_rank
    sib_cw = send(cw, {"core": 1})
    fetched, slot_id, outgoing, sib_cw = lax.optimization_barrier((fetched, slot_id, docs, sib_cw))
    own = fetched.reshape(slab_count * slot_cap, width).at[slot_id].get(mode="promise_in_bounds")

    sib_docs = send(outgoing, {"core": 1})
    column, first, last = ("z", "z"), ("x", "y"), ("y", "x")
    own = jnp.concatenate([own] + [along(own, column, -d) for d in (1, 2, 3)], axis=0)
    own = jnp.concatenate([own] + [along(own, first, -d) for d in (1, 2, 3)], axis=0)
    after, before = along(own, last, -1), along(own, last, -3)
    size = docs.shape[0]
    half = size // 2
    ga, own_docs, sib_low = loading_gains(
        own, [(docs, 0, size, cw), (sib_docs, 0, half, sib_cw)], "gains_near"
    )
    outgoing, ga = lax.optimization_barrier((own, ga))
    across = along(outgoing, last, -2)
    outgoing, sib_low = lax.optimization_barrier((outgoing, sib_low))
    gb, sib_high = loading_gains(
        outgoing, [(sib_docs, half, size, sib_cw)], "gains_near_rest", held=(own_docs, sib_low)
    )
    after, before, gb = lax.optimization_barrier((after, before, gb))
    parts = [(own_docs, 0, cw), (sib_low, 0, sib_cw), (sib_high, half, sib_cw)]
    g1 = gains_of([after, before], parts, "gains_next")
    across, g1 = lax.optimization_barrier((across, g1))
    g2 = gains_of([across], parts, "gains_far")
    ga, gb, g1, g2 = lax.optimization_barrier((ga, gb, g1, g2))
    g0, g1, g2 = jnp.sum(ga + gb, axis=0), jnp.sum(g1, axis=0), jnp.sum(g2, axis=0)
    n = own.shape[0]
    gains = jnp.concatenate([g0, g1[:n], g2, g1[n:]]).reshape(64, share_len)

    my_z, my_x, my_y = slab >> 2, (slab & 2) + (loop & 1), loop >> 1
    to = jnp.arange(64, dtype=jnp.int32)
    to_z, to_x, to_y = to >> 4, ((to >> 2) & 2) + (to & 1), (to >> 1) & 3
    to_z, to_x, to_y = (to_z - my_z) & 3, (to_x - my_x) & 3, (to_y - my_y) & 3
    rel = jnp.where(slab & 1 == 0, to_y * 16 + to_x * 4, to_x * 16 + to_y * 4) + to_z
    pick = rel[:, None] == jnp.arange(64, dtype=jnp.int32)[None, :]
    terms = jnp.sum(jnp.where(pick[:, :, None], gains[None, :, :], 0.0), axis=1)
    groups = [[i for i in range(128) if place(i)[3] == core] for core in range(2)]
    terms = lax.all_to_all(terms, AXES, split_axis=0, concat_axis=0, tiled=True, axis_index_groups=groups)
    return jnp.sum(terms, axis=0).reshape(1, 1, share_len)


def solution(mesh):
    placed = (
        P("slab", "loop", None, None),
        P("slab", "loop", None, None),
        P("slab", "loop", None),
        P("slab", "loop", None, None),
        P("slab", "loop", None),
        P("slab", "loop", None),
    )
    return jax.shard_map(
        body, mesh=mesh, in_specs=placed, out_specs=P("slab", "loop", None), check_vma=False
    )
```

```python
import functools

import jax
import jax.numpy as jnp
from jax import lax
from jax.experimental import pallas as pl
from jax.experimental.pallas import tpu as pltpu
from jax.sharding import PartitionSpec as P

AXES = ("slab", "loop")
RING = 4
TILE = 512
LOAD_TILE = 256
AHEAD = 3


def place(index):
    slab, loop = divmod(index, 8)
    z, rest = divmod(slab, 4)
    hi, core = divmod(rest, 2)
    y, lo = divmod(loop, 2)
    return z, hi * 2 + lo, y, core


def index_of(z, x, y, core):
    return ((z * 2 + x // 2) * 2 + core) * 8 + y * 2 + x % 2


def moves(*steps):
    pairs = []
    for source in range(128):
        z, x, y, core = place(source)
        step = dict(steps[core % len(steps)])
        z, x, y = z + step.get("z", 0), x + step.get("x", 0), y + step.get("y", 0)
        pairs.append((source, index_of(z % RING, x % RING, y % RING, core ^ step.get("core", 0))))
    return pairs


def send(value, *steps):
    return lax.ppermute(value, AXES, moves(*steps))


def along(value, axes, distance):
    return send(value, *({axis: distance} for axis in axes))


def add_terms(cand, docs, cw, out_ref, start, doc_at, tile=TILE):
    scores = lax.dot_general(
        docs[pl.ds(start, tile), :], cand[...], (((1,), (1,)), ((), ())), preferred_element_type=jnp.float32
    )
    columns = cw[:, pl.ds(doc_at, tile)].T
    term = columns[:, 1:2] * jnp.maximum(scores - columns[:, 0:1], 0.0)
    out_ref[...] += jnp.sum(term.reshape(tile // 8, 8, term.shape[1]), axis=0)


def pack(pieces, cand):
    at = 0
    for piece in pieces:
        rows = piece.shape[0]
        cand[at : at + rows, :] = piece[...]
        at += rows


def load_kernel(docs_hbm, after, docs, arrived):
    size = docs.shape[0] // arrived.shape[0]
    copies = [
        pltpu.make_async_copy(
            docs_hbm.at[i * size : (i + 1) * size], docs.at[i * size : (i + 1) * size], arrived.at[i]
        )
        for i in range(arrived.shape[0])
    ]
    for copy in copies:
        copy.start()
    for copy in copies:
        copy.wait()


def load(docs, after, name):
    return pl.pallas_call(
        load_kernel,
        in_specs=[pl.BlockSpec(memory_space=pltpu.HBM), pl.BlockSpec(memory_space=pltpu.VMEM)],
        out_specs=pl.BlockSpec(memory_space=pltpu.VMEM),
        out_shape=pltpu.VMEM(docs.shape, docs.dtype),
        scratch_shapes=[pltpu.SemaphoreType.DMA((4,))],
        compiler_params=pltpu.CompilerParams(vmem_limit_bytes=2 * 2**20),
        cost_estimate=pl.CostEstimate(flops=0, bytes_accessed=docs.size * 2, transcendentals=0),
        name=name,
    )(pltpu.with_memory_space_constraint(docs, pltpu.HBM), after)


def loading_kernel(cand, docs_hbm, cw, *refs):
    out_ref, docs, arrived = refs[-3:]
    steps = docs_hbm.shape[0] // LOAD_TILE

    def copy(i):
        rows = pl.ds(pl.multiple_of(i * LOAD_TILE, LOAD_TILE), LOAD_TILE)
        return pltpu.make_async_copy(docs_hbm.at[rows], docs.at[rows], arrived.at[i])

    for i in range(AHEAD):
        copy(i).start()
    out_ref[...] = jnp.zeros_like(out_ref)

    def step(i, carry):
        @pl.when(i + AHEAD < steps)
        def _():
            copy(i + AHEAD).start()

        copy(i).wait()
        start = pl.multiple_of(i * LOAD_TILE, LOAD_TILE)
        add_terms(cand, docs, cw, out_ref, start, start, LOAD_TILE)
        return carry

    lax.fori_loop(0, steps, step, 0)


def loading_gains(cand, docs, cw, name, held=()):
    rows, width = cand.shape
    in_vmem = pl.BlockSpec(memory_space=pltpu.VMEM)
    return pl.pallas_call(
        loading_kernel,
        in_specs=[in_vmem, pl.BlockSpec(memory_space=pltpu.HBM), in_vmem] + [in_vmem] * len(held),
        out_specs=[in_vmem] * 2,
        out_shape=[jax.ShapeDtypeStruct((8, rows), jnp.float32), pltpu.VMEM(docs.shape, docs.dtype)],
        scratch_shapes=[pltpu.SemaphoreType.DMA((docs.shape[0] // LOAD_TILE,))],
        compiler_params=pltpu.CompilerParams(vmem_limit_bytes=8 * 2**20),
        cost_estimate=pl.CostEstimate(
            flops=5 * docs.shape[0] * rows * width, bytes_accessed=0, transcendentals=0
        ),
        name=name,
    )(cand, pltpu.with_memory_space_constraint(docs, pltpu.HBM), cw, *held)


def gain_kernel(count, lows, *refs):
    pieces = refs[:count]
    docs, cws = refs[count : count + len(lows)], refs[count + len(lows) : count + 2 * len(lows)]
    out_ref = refs[count + 2 * len(lows)]
    if count > 1:
        cand = refs[-1]
        pack(pieces, cand)
    else:
        (cand,) = pieces
    out_ref[...] = jnp.zeros_like(out_ref)
    for part, low in enumerate(lows):
        for start in range(0, docs[part].shape[0], TILE):
            add_terms(cand, docs[part], cws[part], out_ref, start, low + start)


def gains_of(pieces, parts, name):
    count = len(pieces)
    rows, width = sum(p.shape[0] for p in pieces), pieces[0].shape[1]
    docs = sum(part[0].shape[0] for part in parts)
    in_vmem = pl.BlockSpec(memory_space=pltpu.VMEM)
    return pl.pallas_call(
        functools.partial(gain_kernel, count, tuple(part[1] for part in parts)),
        in_specs=[in_vmem] * (count + 2 * len(parts)),
        out_specs=in_vmem,
        out_shape=jax.ShapeDtypeStruct((8, rows), jnp.float32),
        scratch_shapes=[pltpu.VMEM((rows, width), jnp.bfloat16)] if count > 1 else [],
        compiler_params=pltpu.CompilerParams(vmem_limit_bytes=8 * 2**20),
        cost_estimate=pl.CostEstimate(flops=5 * docs * rows * width, bytes_accessed=0, transcendentals=0),
        name=name,
    )(*pieces, *[part[0] for part in parts], *[part[2] for part in parts])


def answer_kernel(me, asked, pool, out_ref, picked):
    askers = asked.shape[0]
    place_of = lax.broadcasted_iota(jnp.int32, asked.shape[1:], 0) * 65536
    for a in range(askers):
        named = asked[a]
        mine = (named >> 16) == me[0]
        key = place_of + (named & 65535)
        first = jnp.min(jnp.where(mine, key, 2**30), axis=0, keepdims=True)
        last = jnp.max(jnp.where(mine, key, 0), axis=0, keepdims=True)
        picked[2 * a : 2 * a + 1, :] = first & 65535
        picked[2 * a + 1 : 2 * a + 2, :] = last & 65535
    lanes = lax.broadcasted_iota(jnp.int32, picked.shape, 1)
    rows = picked[...]
    onehot = jnp.concatenate(
        [(rows == lanes + base).astype(jnp.float32) for base in range(0, pool.shape[0], 128)], axis=1
    ).astype(jnp.bfloat16)
    found = jnp.dot(onehot, pool[...], preferred_element_type=jnp.float32)
    for a in range(askers):
        out_ref[a] = found[2 * a : 2 * a + 2, :].astype(out_ref.dtype)


def answer(me, asked, pool):
    in_vmem = pl.BlockSpec(memory_space=pltpu.VMEM)
    askers, width = asked.shape[0], pool.shape[1]
    return pl.pallas_call(
        answer_kernel,
        in_specs=[pl.BlockSpec(memory_space=pltpu.SMEM), in_vmem, in_vmem],
        out_specs=in_vmem,
        out_shape=jax.ShapeDtypeStruct((askers, 2, width), pool.dtype),
        scratch_shapes=[pltpu.VMEM((2 * askers, 128), jnp.int32)],
        compiler_params=pltpu.CompilerParams(vmem_limit_bytes=10 * 2**20),
        name="answer",
    )(me, asked, pool)


def body(doc_pool, cand_owner, cand_row, elements, coverage, elem_weight):
    share_len = cand_row.shape[2]
    width = doc_pool.shape[3]
    slab_count = 16
    slot_cap = 2
    pool_local = doc_pool.reshape(doc_pool.shape[2], width)
    owner_ids = cand_owner.reshape(share_len)
    row_ids = cand_row.reshape(share_len)
    docs = elements.reshape(elements.shape[2], width)
    scale_up = float(width) ** 0.5
    element_total = float(docs.shape[0] * 128)
    cw = jnp.stack(
        [coverage.reshape(-1) * scale_up, elem_weight.reshape(-1) * (1.0 / (scale_up * element_total))]
    )
    cw = jnp.pad(cw, ((0, 6), (0, 0)))

    slab, loop = lax.axis_index("slab"), lax.axis_index("loop")
    named = jnp.broadcast_to((owner_ids * 65536 + row_ids)[None, :, None], (slab_count, share_len, 128))
    asked = lax.all_to_all(named, "slab", split_axis=0, concat_axis=0, tiled=True)
    rows_out = answer(slab.reshape(1), asked, load(pool_local, cw, "load_pool"))
    rows_out, owner_ids = lax.optimization_barrier((rows_out, owner_ids))
    fetched = lax.all_to_all(rows_out, "slab", split_axis=0, concat_axis=0, tiled=True)
    positions = jnp.arange(share_len, dtype=jnp.int32)
    same_owner = owner_ids[:, None] == owner_ids[None, :]
    earlier = positions[None, :] < positions[:, None]
    slot_rank = jnp.sum((same_owner & earlier).astype(jnp.int32), axis=1)
    slot_id = owner_ids * slot_cap + slot_rank
    sib_cw = send(cw, {"core": 1})
    fetched, slot_id, outgoing, sib_cw = lax.optimization_barrier((fetched, slot_id, docs, sib_cw))
    own = fetched.reshape(slab_count * slot_cap, width).at[slot_id].get(mode="promise_in_bounds")

    sib_docs = send(outgoing, {"core": 1})
    column, first, last = ("z", "z"), ("x", "y"), ("y", "x")
    own = jnp.concatenate([own] + [along(own, column, -d) for d in (1, 2, 3)], axis=0)
    beside = [along(own, first, -d) for d in (1, 2, 3)]
    own_docs = load(docs, own, "load_own")
    own, own_docs, *beside = lax.optimization_barrier((own, own_docs, *beside))
    own = jnp.concatenate([own] + beside, axis=0)
    after, before = along(own, last, -1), along(own, last, -3)
    ga = gains_of([own], [(own_docs, 0, cw)], "gains_near_own")
    sib_docs, ga = lax.optimization_barrier((sib_docs, ga))
    gb, sib_docs = loading_gains(own, sib_docs, sib_cw, "gains_near_sib", held=(own_docs,))
    after, before, gb = lax.optimization_barrier((after, before, gb))
    half = own.shape[0] // 2
    across = [along(after[:half], last, -1), along(before[half:], last, -3)]
    parts = [(own_docs, 0, cw), (sib_docs, 0, sib_cw)]
    g1 = gains_of([after, before], parts, "gains_next")
    *across, g1 = lax.optimization_barrier((*across, g1))
    g2 = gains_of(across, parts, "gains_far")
    ga, gb, g1, g2 = lax.optimization_barrier((ga, gb, g1, g2))
    g0, g1, g2 = jnp.sum(ga + gb, axis=0), jnp.sum(g1, axis=0), jnp.sum(g2, axis=0)
    n = own.shape[0]
    gains = jnp.concatenate([g0, g1[:n], g2, g1[n:]]).reshape(64, share_len)

    my_z, my_x, my_y = slab >> 2, (slab & 2) + (loop & 1), loop >> 1
    to = jnp.arange(64, dtype=jnp.int32)
    to_z, to_x, to_y = to >> 4, ((to >> 2) & 2) + (to & 1), (to >> 1) & 3
    to_z, to_x, to_y = (to_z - my_z) & 3, (to_x - my_x) & 3, (to_y - my_y) & 3
    rel = jnp.where(slab & 1 == 0, to_y * 16 + to_x * 4, to_x * 16 + to_y * 4) + to_z
    pick = rel[:, None] == jnp.arange(64, dtype=jnp.int32)[None, :]
    terms = jnp.sum(jnp.where(pick[:, :, None], gains[None, :, :], 0.0), axis=1)
    groups = [[i for i in range(128) if place(i)[3] == core] for core in range(2)]
    terms = lax.all_to_all(terms, AXES, split_axis=0, concat_axis=0, tiled=True, axis_index_groups=groups)
    return jnp.sum(terms, axis=0).reshape(1, 1, share_len)


def solution(mesh):
    placed = (
        P("slab", "loop", None, None),
        P("slab", "loop", None, None),
        P("slab", "loop", None),
        P("slab", "loop", None, None),
        P("slab", "loop", None),
        P("slab", "loop", None),
    )
    return jax.shard_map(
        body, mesh=mesh, in_specs=placed, out_specs=P("slab", "loop", None), check_vma=False
    )
```

```python
import functools

import jax
import jax.numpy as jnp
from jax import lax
from jax.experimental import pallas as pl
from jax.experimental.pallas import tpu as pltpu
from jax.sharding import PartitionSpec as P

AXES = ("slab", "loop")
RING = 4
TILE = 512


def place(index):
    slab, loop = divmod(index, 8)
    z, rest = divmod(slab, 4)
    hi, core = divmod(rest, 2)
    y, lo = divmod(loop, 2)
    return z, hi * 2 + lo, y, core


def index_of(z, x, y, core):
    return ((z * 2 + x // 2) * 2 + core) * 8 + y * 2 + x % 2


def moves(*steps):
    pairs = []
    for source in range(128):
        z, x, y, core = place(source)
        step = dict(steps[core % len(steps)])
        z, x, y = z + step.get("z", 0), x + step.get("x", 0), y + step.get("y", 0)
        pairs.append((source, index_of(z % RING, x % RING, y % RING, core ^ step.get("core", 0))))
    return pairs


def send(value, *steps):
    return lax.ppermute(value, AXES, moves(*steps))


def along(value, axes, distance):
    return send(value, *({axis: distance} for axis in axes))


def add_terms(cand, docs, cw, out_ref, start, doc_at, tile=TILE):
    scores = lax.dot_general(
        docs[pl.ds(start, tile), :], cand[...], (((1,), (1,)), ((), ())), preferred_element_type=jnp.float32
    )
    columns = cw[:, pl.ds(doc_at, tile)].T
    term = columns[:, 1:2] * jnp.maximum(scores - columns[:, 0:1], 0.0)
    out_ref[...] += jnp.sum(term.reshape(tile // 8, 8, term.shape[1]), axis=0)


def pack(pieces, cand):
    at = 0
    for piece in pieces:
        rows = piece.shape[0]
        cand[at : at + rows, :] = piece[...]
        at += rows


def load_kernel(docs_hbm, after, docs, arrived):
    size = docs.shape[0] // arrived.shape[0]
    copies = [
        pltpu.make_async_copy(
            docs_hbm.at[i * size : (i + 1) * size], docs.at[i * size : (i + 1) * size], arrived.at[i]
        )
        for i in range(arrived.shape[0])
    ]
    for copy in copies:
        copy.start()
    for copy in copies:
        copy.wait()


def load(docs, after, name):
    return pl.pallas_call(
        load_kernel,
        in_specs=[pl.BlockSpec(memory_space=pltpu.HBM), pl.BlockSpec(memory_space=pltpu.VMEM)],
        out_specs=pl.BlockSpec(memory_space=pltpu.VMEM),
        out_shape=pltpu.VMEM(docs.shape, docs.dtype),
        scratch_shapes=[pltpu.SemaphoreType.DMA((4,))],
        compiler_params=pltpu.CompilerParams(vmem_limit_bytes=2 * 2**20),
        cost_estimate=pl.CostEstimate(flops=0, bytes_accessed=docs.size * 2, transcendentals=0),
        name=name,
    )(pltpu.with_memory_space_constraint(docs, pltpu.HBM), after)


def loading_kernel(count, *refs):
    pieces = refs[:count]
    own_docs, sib_hbm, own_cw, sib_cw, out_ref, sib_docs, cand, arrived = refs[count:]
    copies = [
        pltpu.make_async_copy(
            sib_hbm.at[start : start + TILE], sib_docs.at[start : start + TILE], arrived.at[start // TILE]
        )
        for start in range(0, sib_docs.shape[0], TILE)
    ]
    for copy in copies:
        copy.start()
    pack(pieces, cand)
    out_ref[...] = jnp.zeros_like(out_ref)
    for start in range(0, own_docs.shape[0], TILE):
        add_terms(cand, own_docs, own_cw, out_ref, start, start)
    for copy in copies:
        copy.wait()
    for start in range(0, sib_docs.shape[0], TILE):
        add_terms(cand, sib_docs, sib_cw, out_ref, start, start)


def loading_gains(pieces, own_docs, sib_docs, own_cw, sib_cw, name):
    count = len(pieces)
    rows, width = sum(p.shape[0] for p in pieces), pieces[0].shape[1]
    in_vmem = pl.BlockSpec(memory_space=pltpu.VMEM)
    in_hbm = pl.BlockSpec(memory_space=pltpu.HBM)
    return pl.pallas_call(
        functools.partial(loading_kernel, count),
        in_specs=[in_vmem] * (count + 1) + [in_hbm] + [in_vmem] * 2,
        out_specs=[in_vmem] * 2,
        out_shape=[
            jax.ShapeDtypeStruct((8, rows), jnp.float32),
            pltpu.VMEM(sib_docs.shape, sib_docs.dtype),
        ],
        scratch_shapes=[
            pltpu.VMEM((rows, width), jnp.bfloat16),
            pltpu.SemaphoreType.DMA((sib_docs.shape[0] // TILE,)),
        ],
        compiler_params=pltpu.CompilerParams(vmem_limit_bytes=8 * 2**20),
        cost_estimate=pl.CostEstimate(
            flops=5 * sib_docs.shape[0] * rows * width, bytes_accessed=0, transcendentals=0
        ),
        name=name,
    )(*pieces, own_docs, pltpu.with_memory_space_constraint(sib_docs, pltpu.HBM), own_cw, sib_cw)


def gain_kernel(count, lows, *refs):
    pieces = refs[:count]
    docs, cws = refs[count : count + len(lows)], refs[count + len(lows) : count + 2 * len(lows)]
    out_ref = refs[count + 2 * len(lows)]
    if count > 1:
        cand = refs[-1]
        pack(pieces, cand)
    else:
        (cand,) = pieces
    out_ref[...] = jnp.zeros_like(out_ref)
    for part, low in enumerate(lows):
        for start in range(0, docs[part].shape[0], TILE):
            add_terms(cand, docs[part], cws[part], out_ref, start, low + start)


def gains_of(pieces, parts, name):
    count = len(pieces)
    rows, width = sum(p.shape[0] for p in pieces), pieces[0].shape[1]
    docs = sum(part[0].shape[0] for part in parts)
    in_vmem = pl.BlockSpec(memory_space=pltpu.VMEM)
    return pl.pallas_call(
        functools.partial(gain_kernel, count, tuple(part[1] for part in parts)),
        in_specs=[in_vmem] * (count + 2 * len(parts)),
        out_specs=in_vmem,
        out_shape=jax.ShapeDtypeStruct((8, rows), jnp.float32),
        scratch_shapes=[pltpu.VMEM((rows, width), jnp.bfloat16)] if count > 1 else [],
        compiler_params=pltpu.CompilerParams(vmem_limit_bytes=8 * 2**20),
        cost_estimate=pl.CostEstimate(flops=5 * docs * rows * width, bytes_accessed=0, transcendentals=0),
        name=name,
    )(*pieces, *[part[0] for part in parts], *[part[2] for part in parts])


def answer_kernel(me, asked, pool, out_ref, picked):
    askers = asked.shape[0]
    place_of = lax.broadcasted_iota(jnp.int32, asked.shape[1:], 0) * 65536
    for a in range(askers):
        named = asked[a]
        mine = (named >> 16) == me[0]
        key = place_of + (named & 65535)
        first = jnp.min(jnp.where(mine, key, 2**30), axis=0, keepdims=True)
        last = jnp.max(jnp.where(mine, key, 0), axis=0, keepdims=True)
        picked[2 * a : 2 * a + 1, :] = first & 65535
        picked[2 * a + 1 : 2 * a + 2, :] = last & 65535
    lanes = lax.broadcasted_iota(jnp.int32, picked.shape, 1)
    rows = picked[...]
    onehot = jnp.concatenate(
        [(rows == lanes + base).astype(jnp.float32) for base in range(0, pool.shape[0], 128)], axis=1
    ).astype(jnp.bfloat16)
    found = jnp.dot(onehot, pool[...], preferred_element_type=jnp.float32)
    for a in range(askers):
        out_ref[a] = found[2 * a : 2 * a + 2, :].astype(out_ref.dtype)


def answer(me, asked, pool):
    in_vmem = pl.BlockSpec(memory_space=pltpu.VMEM)
    askers, width = asked.shape[0], pool.shape[1]
    return pl.pallas_call(
        answer_kernel,
        in_specs=[pl.BlockSpec(memory_space=pltpu.SMEM), in_vmem, in_vmem],
        out_specs=in_vmem,
        out_shape=jax.ShapeDtypeStruct((askers, 2, width), pool.dtype),
        scratch_shapes=[pltpu.VMEM((2 * askers, 128), jnp.int32)],
        compiler_params=pltpu.CompilerParams(vmem_limit_bytes=10 * 2**20),
        name="answer",
    )(me, asked, pool)


def body(doc_pool, cand_owner, cand_row, elements, coverage, elem_weight):
    share_len = cand_row.shape[2]
    width = doc_pool.shape[3]
    slab_count = 16
    slot_cap = 2
    pool_local = doc_pool.reshape(doc_pool.shape[2], width)
    owner_ids = cand_owner.reshape(share_len)
    row_ids = cand_row.reshape(share_len)
    docs = elements.reshape(elements.shape[2], width)
    scale_up = float(width) ** 0.5
    element_total = float(docs.shape[0] * 128)
    cw = jnp.stack(
        [coverage.reshape(-1) * scale_up, elem_weight.reshape(-1) * (1.0 / (scale_up * element_total))]
    )
    cw = jnp.pad(cw, ((0, 6), (0, 0)))

    slab, loop = lax.axis_index("slab"), lax.axis_index("loop")
    named = jnp.broadcast_to((owner_ids * 65536 + row_ids)[None, :, None], (slab_count, share_len, 128))
    asked = lax.all_to_all(named, "slab", split_axis=0, concat_axis=0, tiled=True)
    rows_out = answer(slab.reshape(1), asked, load(pool_local, cw, "load_pool"))
    rows_out, owner_ids = lax.optimization_barrier((rows_out, owner_ids))
    fetched = lax.all_to_all(rows_out, "slab", split_axis=0, concat_axis=0, tiled=True)
    positions = jnp.arange(share_len, dtype=jnp.int32)
    same_owner = owner_ids[:, None] == owner_ids[None, :]
    earlier = positions[None, :] < positions[:, None]
    slot_rank = jnp.sum((same_owner & earlier).astype(jnp.int32), axis=1)
    slot_id = owner_ids * slot_cap + slot_rank
    sib_cw = send(cw, {"core": 1})
    fetched, slot_id, outgoing, sib_cw = lax.optimization_barrier((fetched, slot_id, docs, sib_cw))
    own = fetched.reshape(slab_count * slot_cap, width).at[slot_id].get(mode="promise_in_bounds")

    sib_docs = send(outgoing, {"core": 1})
    column, first, last = ("z", "z"), ("x", "y"), ("y", "x")
    own = jnp.concatenate([own] + [along(own, column, -d) for d in (1, 2, 3)], axis=0)
    beside = [along(own, first, -d) for d in (1, 2, 3)]
    low = jnp.concatenate([own, beside[0]], axis=0)
    high = jnp.concatenate(beside[1:], axis=0)
    after_low, before_high = along(low, last, -1), along(high, last, -3)
    own_docs = load(docs, low, "load_own")
    low_again, high_again, own_docs = lax.optimization_barrier((low, high, own_docs))
    after_high, before_low = along(high_again, last, -1), along(low_again, last, -3)
    far_low, far_high = along(after_low, last, -1), along(before_high, last, -3)
    g1, sib_docs = loading_gains(
        [low_again, high_again, after_low, before_high], own_docs, sib_docs, cw, sib_cw, "gains_near"
    )
    after_high, before_low, far_low, far_high, g1 = lax.optimization_barrier(
        (after_high, before_low, far_low, far_high, g1)
    )
    parts = [(own_docs, 0, cw), (sib_docs, 0, sib_cw)]
    g2 = gains_of([after_high, before_low, far_low, far_high], parts, "gains_far")
    g1, g2 = lax.optimization_barrier((g1, g2))
    n = low.shape[0]
    g1, g2 = jnp.sum(g1, axis=0).reshape(4, n), jnp.sum(g2, axis=0).reshape(4, n)
    gains = jnp.stack([g1[0], g1[1], g1[2], g2[0], g2[2], g2[3], g2[1], g1[3]]).reshape(64, share_len)

    my_z, my_x, my_y = slab >> 2, (slab & 2) + (loop & 1), loop >> 1
    to = jnp.arange(64, dtype=jnp.int32)
    to_z, to_x, to_y = to >> 4, ((to >> 2) & 2) + (to & 1), (to >> 1) & 3
    to_z, to_x, to_y = (to_z - my_z) & 3, (to_x - my_x) & 3, (to_y - my_y) & 3
    rel = jnp.where(slab & 1 == 0, to_y * 16 + to_x * 4, to_x * 16 + to_y * 4) + to_z
    pick = rel[:, None] == jnp.arange(64, dtype=jnp.int32)[None, :]
    terms = jnp.sum(jnp.where(pick[:, :, None], gains[None, :, :], 0.0), axis=1)
    groups = [[i for i in range(128) if place(i)[3] == core] for core in range(2)]
    terms = lax.all_to_all(terms, AXES, split_axis=0, concat_axis=0, tiled=True, axis_index_groups=groups)
    return jnp.sum(terms, axis=0).reshape(1, 1, share_len)


def solution(mesh):
    placed = (
        P("slab", "loop", None, None),
        P("slab", "loop", None, None),
        P("slab", "loop", None),
        P("slab", "loop", None, None),
        P("slab", "loop", None),
        P("slab", "loop", None),
    )
    return jax.shard_map(
        body, mesh=mesh, in_specs=placed, out_specs=P("slab", "loop", None), check_vma=False
    )
```

```python
import functools

import jax
import jax.numpy as jnp
from jax import lax
from jax.experimental import pallas as pl
from jax.experimental.pallas import tpu as pltpu
from jax.sharding import PartitionSpec as P

AXES = ("slab", "loop")
RING = 4
TILE = 512


def place(index):
    slab, loop = divmod(index, 8)
    z, rest = divmod(slab, 4)
    hi, core = divmod(rest, 2)
    y, lo = divmod(loop, 2)
    return z, hi * 2 + lo, y, core


def index_of(z, x, y, core):
    return ((z * 2 + x // 2) * 2 + core) * 8 + y * 2 + x % 2


def moves(*steps):
    pairs = []
    for source in range(128):
        z, x, y, core = place(source)
        step = dict(steps[core % len(steps)])
        z, x, y = z + step.get("z", 0), x + step.get("x", 0), y + step.get("y", 0)
        pairs.append((source, index_of(z % RING, x % RING, y % RING, core ^ step.get("core", 0))))
    return pairs


def send(value, *steps):
    return lax.ppermute(value, AXES, moves(*steps))


def along(value, axes, distance):
    return send(value, *({axis: distance} for axis in axes))


def add_terms(cand, docs, cw, out_ref, start, doc_at, tile=TILE):
    scores = lax.dot_general(
        docs[pl.ds(start, tile), :], cand[...], (((1,), (1,)), ((), ())), preferred_element_type=jnp.float32
    )
    columns = cw[:, pl.ds(doc_at, tile)].T
    term = columns[:, 1:2] * jnp.maximum(scores - columns[:, 0:1], 0.0)
    out_ref[...] += jnp.sum(term.reshape(tile // 8, 8, term.shape[1]), axis=0)


def pack(pieces, cand):
    at = 0
    for piece in pieces:
        rows = piece.shape[0]
        cand[at : at + rows, :] = piece[...]
        at += rows


def load_kernel(docs_hbm, after, docs, arrived):
    size = docs.shape[0] // arrived.shape[0]
    copies = [
        pltpu.make_async_copy(
            docs_hbm.at[i * size : (i + 1) * size], docs.at[i * size : (i + 1) * size], arrived.at[i]
        )
        for i in range(arrived.shape[0])
    ]
    for copy in copies:
        copy.start()
    for copy in copies:
        copy.wait()


def load(docs, after, name):
    return pl.pallas_call(
        load_kernel,
        in_specs=[pl.BlockSpec(memory_space=pltpu.HBM), pl.BlockSpec(memory_space=pltpu.VMEM)],
        out_specs=pl.BlockSpec(memory_space=pltpu.VMEM),
        out_shape=pltpu.VMEM(docs.shape, docs.dtype),
        scratch_shapes=[pltpu.SemaphoreType.DMA((4,))],
        compiler_params=pltpu.CompilerParams(vmem_limit_bytes=2 * 2**20),
        cost_estimate=pl.CostEstimate(flops=0, bytes_accessed=docs.size * 2, transcendentals=0),
        name=name,
    )(pltpu.with_memory_space_constraint(docs, pltpu.HBM), after)


def loading_kernel(count, *refs):
    pieces = refs[:count]
    own_docs, sib_hbm, own_cw, sib_cw, out_ref, sib_docs, cand, arrived = refs[count:]
    copies = [
        pltpu.make_async_copy(
            sib_hbm.at[start : start + TILE], sib_docs.at[start : start + TILE], arrived.at[start // TILE]
        )
        for start in range(0, sib_docs.shape[0], TILE)
    ]
    for copy in copies:
        copy.start()
    pack(pieces, cand)
    out_ref[...] = jnp.zeros_like(out_ref)
    rows = cand.shape[0]
    new = pl.ds(rows // 2, rows // 2)
    for start in range(0, own_docs.shape[0], TILE):
        add_terms(cand.at[new, :], own_docs, own_cw, out_ref.at[:, new], start, start)
    for copy in copies:
        copy.wait()
    for start in range(0, sib_docs.shape[0], TILE):
        add_terms(cand, sib_docs, sib_cw, out_ref, start, start)


def loading_gains(pieces, own_docs, sib_docs, own_cw, sib_cw, name):
    count = len(pieces)
    rows, width = sum(p.shape[0] for p in pieces), pieces[0].shape[1]
    in_vmem = pl.BlockSpec(memory_space=pltpu.VMEM)
    in_hbm = pl.BlockSpec(memory_space=pltpu.HBM)
    return pl.pallas_call(
        functools.partial(loading_kernel, count),
        in_specs=[in_vmem] * (count + 1) + [in_hbm] + [in_vmem] * 2,
        out_specs=[in_vmem] * 2,
        out_shape=[
            jax.ShapeDtypeStruct((8, rows), jnp.float32),
            pltpu.VMEM(sib_docs.shape, sib_docs.dtype),
        ],
        scratch_shapes=[
            pltpu.VMEM((rows, width), jnp.bfloat16),
            pltpu.SemaphoreType.DMA((sib_docs.shape[0] // TILE,)),
        ],
        compiler_params=pltpu.CompilerParams(vmem_limit_bytes=8 * 2**20),
        cost_estimate=pl.CostEstimate(
            flops=5 * sib_docs.shape[0] * rows * width, bytes_accessed=0, transcendentals=0
        ),
        name=name,
    )(*pieces, own_docs, pltpu.with_memory_space_constraint(sib_docs, pltpu.HBM), own_cw, sib_cw)


def gain_kernel(count, lows, *refs):
    pieces = refs[:count]
    docs, cws = refs[count : count + len(lows)], refs[count + len(lows) : count + 2 * len(lows)]
    out_ref = refs[count + 2 * len(lows)]
    if count > 1:
        cand = refs[-1]
        pack(pieces, cand)
    else:
        (cand,) = pieces
    out_ref[...] = jnp.zeros_like(out_ref)
    for part, low in enumerate(lows):
        for start in range(0, docs[part].shape[0], TILE):
            add_terms(cand, docs[part], cws[part], out_ref, start, low + start)


def gains_of(pieces, parts, name):
    count = len(pieces)
    rows, width = sum(p.shape[0] for p in pieces), pieces[0].shape[1]
    docs = sum(part[0].shape[0] for part in parts)
    in_vmem = pl.BlockSpec(memory_space=pltpu.VMEM)
    return pl.pallas_call(
        functools.partial(gain_kernel, count, tuple(part[1] for part in parts)),
        in_specs=[in_vmem] * (count + 2 * len(parts)),
        out_specs=in_vmem,
        out_shape=jax.ShapeDtypeStruct((8, rows), jnp.float32),
        scratch_shapes=[pltpu.VMEM((rows, width), jnp.bfloat16)] if count > 1 else [],
        compiler_params=pltpu.CompilerParams(vmem_limit_bytes=8 * 2**20),
        cost_estimate=pl.CostEstimate(flops=5 * docs * rows * width, bytes_accessed=0, transcendentals=0),
        name=name,
    )(*pieces, *[part[0] for part in parts], *[part[2] for part in parts])


def answer_kernel(me, asked, pool, out_ref, picked):
    askers = asked.shape[0]
    place_of = lax.broadcasted_iota(jnp.int32, asked.shape[1:], 0) * 65536
    for a in range(askers):
        named = asked[a]
        mine = (named >> 16) == me[0]
        key = place_of + (named & 65535)
        first = jnp.min(jnp.where(mine, key, 2**30), axis=0, keepdims=True)
        last = jnp.max(jnp.where(mine, key, 0), axis=0, keepdims=True)
        picked[2 * a : 2 * a + 1, :] = first & 65535
        picked[2 * a + 1 : 2 * a + 2, :] = last & 65535
    lanes = lax.broadcasted_iota(jnp.int32, picked.shape, 1)
    rows = picked[...]
    onehot = jnp.concatenate(
        [(rows == lanes + base).astype(jnp.float32) for base in range(0, pool.shape[0], 128)], axis=1
    ).astype(jnp.bfloat16)
    found = jnp.dot(onehot, pool[...], preferred_element_type=jnp.float32)
    for a in range(askers):
        out_ref[a] = found[2 * a : 2 * a + 2, :].astype(out_ref.dtype)


def answer(me, asked, pool):
    in_vmem = pl.BlockSpec(memory_space=pltpu.VMEM)
    askers, width = asked.shape[0], pool.shape[1]
    return pl.pallas_call(
        answer_kernel,
        in_specs=[pl.BlockSpec(memory_space=pltpu.SMEM), in_vmem, in_vmem],
        out_specs=in_vmem,
        out_shape=jax.ShapeDtypeStruct((askers, 2, width), pool.dtype),
        scratch_shapes=[pltpu.VMEM((2 * askers, 128), jnp.int32)],
        compiler_params=pltpu.CompilerParams(vmem_limit_bytes=10 * 2**20),
        name="answer",
    )(me, asked, pool)


def body(doc_pool, cand_owner, cand_row, elements, coverage, elem_weight):
    share_len = cand_row.shape[2]
    width = doc_pool.shape[3]
    slab_count = 16
    slot_cap = 2
    pool_local = doc_pool.reshape(doc_pool.shape[2], width)
    owner_ids = cand_owner.reshape(share_len)
    row_ids = cand_row.reshape(share_len)
    docs = elements.reshape(elements.shape[2], width)
    scale_up = float(width) ** 0.5
    element_total = float(docs.shape[0] * 128)
    cw = jnp.stack(
        [coverage.reshape(-1) * scale_up, elem_weight.reshape(-1) * (1.0 / (scale_up * element_total))]
    )
    cw = jnp.pad(cw, ((0, 6), (0, 0)))

    slab, loop = lax.axis_index("slab"), lax.axis_index("loop")
    named = jnp.broadcast_to((owner_ids * 65536 + row_ids)[None, :, None], (slab_count, share_len, 128))
    asked = lax.all_to_all(named, "slab", split_axis=0, concat_axis=0, tiled=True)
    rows_out = answer(slab.reshape(1), asked, load(pool_local, cw, "load_pool"))
    rows_out, owner_ids = lax.optimization_barrier((rows_out, owner_ids))
    fetched = lax.all_to_all(rows_out, "slab", split_axis=0, concat_axis=0, tiled=True)
    positions = jnp.arange(share_len, dtype=jnp.int32)
    same_owner = owner_ids[:, None] == owner_ids[None, :]
    earlier = positions[None, :] < positions[:, None]
    slot_rank = jnp.sum((same_owner & earlier).astype(jnp.int32), axis=1)
    slot_id = owner_ids * slot_cap + slot_rank
    sib_cw = send(cw, {"core": 1})
    fetched, slot_id, outgoing, sib_cw = lax.optimization_barrier((fetched, slot_id, docs, sib_cw))
    own = fetched.reshape(slab_count * slot_cap, width).at[slot_id].get(mode="promise_in_bounds")

    sib_docs = send(outgoing, {"core": 1})
    column, first, last = ("z", "z"), ("x", "y"), ("y", "x")
    own = jnp.concatenate([own] + [along(own, column, -d) for d in (1, 2, 3)], axis=0)
    beside = [along(own, first, -d) for d in (1, 2, 3)]
    own_docs = load(docs, own, "load_own")
    own, own_docs, *beside = lax.optimization_barrier((own, own_docs, *beside))
    low = jnp.concatenate([own, beside[0]], axis=0)
    high = jnp.concatenate(beside[1:], axis=0)
    after_low, before_high = along(low, last, -1), along(high, last, -3)
    g0 = gains_of([low, high], [(own_docs, 0, cw)], "gains_own")
    low_again, high_again, g0 = lax.optimization_barrier((low, high, g0))
    after_high, before_low = along(high_again, last, -1), along(low_again, last, -3)
    far_low, far_high = along(after_low, last, -1), along(before_high, last, -3)
    g1, sib_docs = loading_gains(
        [low_again, high_again, after_low, before_high], own_docs, sib_docs, cw, sib_cw, "gains_near"
    )
    after_high, before_low, far_low, far_high, g1 = lax.optimization_barrier(
        (after_high, before_low, far_low, far_high, g1)
    )
    parts = [(own_docs, 0, cw), (sib_docs, 0, sib_cw)]
    g2 = gains_of([after_high, before_low, far_low, far_high], parts, "gains_far")
    g0, g1, g2 = lax.optimization_barrier((g0, g1, g2))
    n = low.shape[0]
    g1 = g1 + jnp.pad(g0, ((0, 0), (0, 2 * n)))
    g1, g2 = jnp.sum(g1, axis=0).reshape(4, n), jnp.sum(g2, axis=0).reshape(4, n)
    gains = jnp.stack([g1[0], g1[1], g1[2], g2[0], g2[2], g2[3], g2[1], g1[3]]).reshape(64, share_len)

    my_z, my_x, my_y = slab >> 2, (slab & 2) + (loop & 1), loop >> 1
    to = jnp.arange(64, dtype=jnp.int32)
    to_z, to_x, to_y = to >> 4, ((to >> 2) & 2) + (to & 1), (to >> 1) & 3
    to_z, to_x, to_y = (to_z - my_z) & 3, (to_x - my_x) & 3, (to_y - my_y) & 3
    rel = jnp.where(slab & 1 == 0, to_y * 16 + to_x * 4, to_x * 16 + to_y * 4) + to_z
    pick = rel[:, None] == jnp.arange(64, dtype=jnp.int32)[None, :]
    terms = jnp.sum(jnp.where(pick[:, :, None], gains[None, :, :], 0.0), axis=1)
    groups = [[i for i in range(128) if place(i)[3] == core] for core in range(2)]
    terms = lax.all_to_all(terms, AXES, split_axis=0, concat_axis=0, tiled=True, axis_index_groups=groups)
    return jnp.sum(terms, axis=0).reshape(1, 1, share_len)


def solution(mesh):
    placed = (
        P("slab", "loop", None, None),
        P("slab", "loop", None, None),
        P("slab", "loop", None),
        P("slab", "loop", None, None),
        P("slab", "loop", None),
        P("slab", "loop", None),
    )
    return jax.shard_map(
        body, mesh=mesh, in_specs=placed, out_specs=P("slab", "loop", None), check_vma=False
    )
```
